32 devices in a mesh: groups: 2 (over y), expert: 16 (over z, x, core), sub: 1.
Axes of the slice: x: 2, y: 2, z: 4, core: 2. Of those that a mesh axis runs over, the one named last changes fastest.
Arguments:
- hidden: bfloat16 [4, 512, 8, 1024], P(None, ('groups', 'expert'), None, 'sub'), parts along dimension 1, may hold values from -6 to 6
- down_weight: bfloat16 [16, 1024, 3584], P('expert', None, 'sub'), may hold values from -0.1875 to 0.1875
- logits: float32 [4, 512, 8], P(None, ('groups', 'expert')), parts along dimension 1, may hold values from -6 to 6
- routes: int32 [4, 512, 8], P(None, ('groups', 'expert')), parts along dimension 1, may hold values from 0 to 15, all different within a row; in each aligned block of 16 rows (0 to 15, 16 to 31, ..., all dimensions but the last counted through in order) at most 16 rows name the same one
- placement: int32 [16], replicated, may hold values from 0 to 15, each once
- pair_slice: int32 [8, 16], P('groups', 'expert'), parts along dimension 0, may hold values from 0 to 31
Outputs:
- mixed: bfloat16 [4, 512, 3584], P(None, ('groups', 'expert'), 'sub'), parts along dimension 1
- swapped: bfloat16 [8, 16, 32, 3584], P('groups', 'expert', None, 'sub'), parts along dimension 0
The draws below stay inside these ranges and needn't reach their ends.
There are 2 independent parts, one for each index of `groups`. The reference program is written for one: setup_inputs(seed, part) draws one part's arguments, and reference() takes and returns one part's arrays. A program takes and returns all parts, laid end to end along the dimension named above; an argument that names none is the same for every part. Nothing has to cross between parts.
Inputs may be any that keep to these rules, and one draw needn't show every extreme that they name: `routes`: each row names 8 different experts. In every aligned block of 16 rows (the tokens of one index of the expert axis in one step) no expert is named by more than 16 rows, a bound that some block reaches. `placement`: A permutation of the experts.
All inputs are finite; a program needn't handle non-finite values.
Results may differ from the reference program's by a relative error of at most 0.0049.
Values may be sent and summed in bfloat16 or wider, within the bound.
A program may use at most 64 MiB of HBM per device.

```python
import math
import jax
import jax.numpy as jnp
import numpy as np
from jax import lax

D = 3584
H = 1024
TOP = 8
STEPS = 4
NSLICE = 32
TOK_DEV = 16
EXPERTS = 16
TOKENS = 256
C = 16
SLICE_ROWS = 32
N_EXPERT = 16


def with_ends(entries, stream_key, least, high):
    longest = entries.shape.index(max(entries.shape))
    spots = []
    for shift in (0, 1):
        where = [jax.random.randint(jax.random.fold_in(stream_key, axis), (), 0, length) for axis, length in enumerate(entries.shape)]
        where[longest] = (where[longest] + shift) % entries.shape[longest]
        spots.append(tuple(where))
    return entries.at[spots[0]].set(least).at[spots[1]].set(high)


def block_scale(key, shape, shards, least, top_value):
    loudness, own = 1.0, jax.random.fold_in(key, 6)
    for axis_at, blocks in shards:
        draws = jnp.exp(jax.random.uniform(jax.random.fold_in(own, axis_at), (blocks,), jnp.float32, least / len(shards), top_value / len(shards)))
        loudness = loudness * jnp.repeat(draws, shape[axis_at] // blocks).reshape([-1 if axis == axis_at else 1 for axis in range(len(shape))])
    return loudness


def shared_out(stream_key, own, number, rows, amount, top, limit, lean):
    ranking = jax.random.permutation(stream_key, amount)
    crowded, ordinary = portions_of(amount, rows * top, limit, lean, True), portions_of(amount, rows * top, limit, lean, False)
    places = jnp.arange(amount)

    def named(tallies, turn):
        used = int((tallies > 0).sum())
        fixed = max(1, used // 4)
        moved = fixed + (places - fixed + turn * (used - fixed)) % max(1, amount - fixed)
        return jnp.zeros((amount,), jnp.int32).at[ranking[jnp.where(places < fixed, places, moved)]].set(jnp.asarray(tallies, jnp.int32))

    tallies = jnp.where(number % 4 == 0, named(crowded, number // 4), named(ordinary, number - number // 4 - 1))
    mixed = jax.random.permutation(jax.random.fold_in(own, 3), amount)
    source_of, taker = mixed[0:amount // 2 * 2:2], mixed[1:amount // 2 * 2:2]
    slack = jnp.minimum(tallies[source_of] - 1, limit - tallies[taker]) // 2
    slack = jnp.where((source_of == ranking[0]) | (taker == ranking[0]) | (tallies[taker] == 0), 0, jnp.maximum(slack, 0))
    moved = jax.random.randint(jax.random.fold_in(own, 4), (amount // 2,), 0, 1 << 20) % (slack + 1)
    tallies = tallies.at[source_of].add(-moved).at[taker].add(moved)
    members = jnp.searchsorted(jnp.cumsum(tallies), jnp.arange(rows * top), side="right").astype(jnp.int32)
    listing = members.reshape(top, rows).T
    listing = listing[jax.random.permutation(jax.random.fold_in(own, 1), rows)]
    turn = jax.random.randint(jax.random.fold_in(own, 2), (rows, 1), 0, top)
    return jnp.take_along_axis(listing, (jnp.arange(top)[None, :] + turn) % top, axis=1)


def portions_of(amount, total, limit, lean, full):
    weights = [(1 << 20) // math.isqrt(standing ** lean) + 1 for standing in range(1, amount + 1)]
    largest = limit if full else min(limit, max(-(-total // amount), total * weights[0] // sum(weights)))
    least = 1 if total - largest >= amount - 1 else 0
    holding, rest = [largest] + [least] * (amount - 1), total - largest - least * (amount - 1)
    while rest > 0:
        movable = [i for i in range(1, amount) if holding[i] < largest] or [i for i in range(1, amount) if holding[i] < limit]
        whole, left = sum([weights[i] for i in movable]), rest
        for i in movable:
            addition = min(limit - holding[i], max(1, left * weights[i] // whole), rest)
            holding[i] = holding[i] + addition
            rest = rest - addition
    return np.array(holding)


def normal_values(own_key, dims, spread, reach, split=(), kind=jnp.bfloat16):
    entries = spread * jax.random.normal(own_key, dims, jnp.float32)
    if split:
        entries = entries * block_scale(own_key, dims, split, -0.22, 0.18)
    return jnp.clip(entries, -reach, reach).astype(kind)


def setup_inputs(seed: int = 0, part: int = 0) -> dict:
    seeds = jax.random.split(jax.random.key(seed), 7)
    part_splits = jax.random.split(jax.random.fold_in(seeds[6], part), 7)
    hidden = normal_values(part_splits[0], (STEPS, TOKENS, TOP, H), 1.0, 6.0, ((1, 16),))
    down_weight = normal_values(seeds[1], (EXPERTS, H, D), H ** -0.5, 0.1875, ((0, 16),))
    logits = normal_values(part_splits[2], (STEPS, TOKENS, TOP), 1.5, 6.0, ((1, 16),), jnp.float32)
    routes_keys = jax.random.split(jax.random.fold_in(part_splits[3], 1), STEPS * TOKENS // TOK_DEV)
    routes_turns = jax.random.permutation(jax.random.fold_in(part_splits[3], 3), STEPS * TOKENS // TOK_DEV)
    routes = jax.vmap(lambda own, number: shared_out(jax.random.fold_in(part_splits[3], 2), own, number, TOK_DEV, EXPERTS, TOP, C, 2))(routes_keys, routes_turns).reshape((STEPS, TOKENS, TOP))
    placement = jax.random.permutation(seeds[4], EXPERTS).astype(jnp.int32)
    pair_slice = with_ends(jax.random.randint(part_splits[5], (STEPS, EXPERTS), 0, NSLICE), jax.random.fold_in(part_splits[5], 1), 0, NSLICE - 1).astype(jnp.int32)
    return dict(hidden=hidden, down_weight=down_weight, logits=logits, routes=routes, placement=placement, pair_slice=pair_slice)


ROUTE_SCALE = 2.5


def expert_pass(buffers, down_weight):
    def one_expert(operands):
        return jnp.dot(operands[0], operands[1], preferred_element_type=jnp.float32).astype(jnp.bfloat16)
    return lax.map(one_expert, (buffers, down_weight))


def reference(hidden, down_weight, logits, routes, placement, pair_slice):
    owners = placement[routes].astype(jnp.int32)
    blocks = owners.reshape(STEPS, N_EXPERT, TOK_DEV * TOP)
    onehot = (blocks[..., None] == jnp.arange(EXPERTS, dtype=jnp.int32)).astype(jnp.int32)
    earlier = (jnp.cumsum(onehot, axis=2) - onehot).astype(jnp.int32)
    slot_of = jnp.sum(earlier * onehot, axis=3).astype(jnp.int32)
    sources = jnp.arange(N_EXPERT, dtype=jnp.int32)[None, :, None]
    position = (sources * C + slot_of).astype(jnp.int32)
    scores = jax.nn.sigmoid(logits)
    gating = ROUTE_SCALE * scores / jnp.sum(scores, axis=-1, keepdims=True)
    outputs = []
    for step in range(STEPS):
        token_rows = hidden[step].reshape(N_EXPERT, TOK_DEV * TOP, H)
        buffers = jnp.zeros((EXPERTS, N_EXPERT * C, H), jnp.bfloat16)
        buffers = buffers.at[blocks[step], position[step]].set(token_rows)
        results = expert_pass(buffers, down_weight)
        picked = results[blocks[step], position[step]].reshape(TOKENS, TOP, D)
        mixed_rows = jnp.sum(gating[step][..., None] * picked.astype(jnp.float32), axis=1)
        outputs.append(mixed_rows.astype(jnp.bfloat16))
    levels = N_EXPERT.bit_length() - 1
    device_index = jnp.arange(EXPERTS, dtype=jnp.int32)
    swapped = []
    for step in range(STEPS):
        swap_bit = levels - 1 - (step % levels)
        partner = jnp.bitwise_xor(device_index, 1 << swap_bit).astype(jnp.int32)
        first_row = (pair_slice[step][partner] * SLICE_ROWS).astype(jnp.int32)
        row_ids = (first_row[:, None] + jnp.arange(SLICE_ROWS, dtype=jnp.int32)[None, :]).astype(jnp.int32)
        swapped.append(down_weight[partner[:, None], row_ids])
    return jnp.stack(outputs), jnp.stack(swapped)
```

```python
import functools
import jax
import jax.numpy as jnp
from jax import lax
from jax.experimental import pallas as pl
from jax.experimental.pallas import tpu as pltpu
from jax.sharding import PartitionSpec as P

MESH = pl.DeviceIdType.MESH
NSLICE = 32
VMEM_BYTES = 60 * 2**20


ROUTE_SCALE = 2.5


def swapped(value, axis, stride):
    mask = 2**stride
    pairs = [(source, source ^ mask) for source in range(lax.axis_size(axis))]
    return lax.ppermute(value, axis, pairs)


def widen_rows(flat_rows):
    return lax.all_gather(flat_rows, "sub", axis=1, tiled=True)


def send_back(results):
    return lax.all_to_all(results, "expert", split_axis=0, concat_axis=0, tiled=True)


def plain_device(hidden, down_weight, logits, routes, placement, pair_slice):
    steps, tok_rows, top_count, hidden_cols = hidden.shape
    devices = lax.axis_size("expert")
    capacity = min(tok_rows, 2 * ((tok_rows * top_count + devices - 1) // devices))
    weights = down_weight[0]
    slice_rows = weights.shape[0] // NSLICE
    expert_ids = jnp.arange(devices, dtype=jnp.int32)
    owners = jnp.sum(jnp.where(routes[..., None] == expert_ids, placement, 0), axis=-1)
    owners = owners.reshape(steps, tok_rows * top_count)
    onehot = (owners[..., None] == expert_ids).astype(jnp.int32)
    earlier = jnp.cumsum(onehot, axis=1) - onehot
    slot_of = jnp.sum(earlier * onehot, axis=2)
    slot_ids = jnp.arange(capacity, dtype=jnp.int32)
    chosen = ((onehot[..., None] == 1) & (slot_of[:, :, None, None] == slot_ids)).astype(
        jnp.bfloat16
    )
    chosen = chosen.reshape(steps, tok_rows * top_count, devices * capacity)
    scores = jax.nn.sigmoid(logits)
    gating = ROUTE_SCALE * scores / jnp.sum(scores, axis=-1, keepdims=True)
    token_rows = widen_rows(hidden.reshape(-1, hidden_cols)).reshape(
        steps, tok_rows * top_count, -1
    )
    levels = devices.bit_length() - 1
    mixed_all = []
    swapped_all = []
    for step in range(steps):
        outgoing = jnp.einsum(
            "qm,qw->mw", chosen[step], token_rows[step], preferred_element_type=jnp.float32
        )
        outgoing = outgoing.astype(jnp.bfloat16).reshape(devices, capacity, -1)
        received = lax.all_to_all(outgoing, "expert", split_axis=0, concat_axis=0, tiled=True)
        source_count, slot_count, columns = received.shape
        flat_rows = received.reshape(source_count * slot_count, columns)
        results = jnp.dot(flat_rows, weights, preferred_element_type=jnp.float32).astype(
            jnp.bfloat16
        )
        returned = send_back(results.reshape(source_count, slot_count, -1))
        per_slot = jnp.dot(
            chosen[step],
            returned.reshape(devices * capacity, -1),
            preferred_element_type=jnp.float32,
        )
        weighted = gating[step][..., None] * per_slot.reshape(tok_rows, top_count, -1)
        mixed_all.append(jnp.sum(weighted, axis=1).astype(jnp.bfloat16))
        swap_bit = levels - 1 - step % levels
        start_row = pair_slice[step, 0] * slice_rows
        own_slice = lax.dynamic_slice_in_dim(weights, start_row, slice_rows, 0)
        traded = swapped(own_slice, "expert", swap_bit)
        swapped_all.append(traded[None])
    return (jnp.stack(mixed_all), jnp.stack(swapped_all))


def kernel(
    n, hidden_hbm, weight_hbm, owners_ref, gating_ref, pair_ref, mixed_ref, swapped_ref,
    hid, weights, outbox, inbox, acc, core_out, core_in, x_out, x_in,
    up_out, up_in, down_out, down_in, swap_out,
    local_sem, hid_send, hid_recv, core_sem, x_sem, up_sem, down_sem, swap_sem,
):
    steps = hid.shape[0]
    rows = hid.shape[1]
    tok = inbox.shape[2]
    top = rows // tok
    width = weights.shape[1]
    tile = 512
    planes = n // 4
    me = lax.axis_index("expert")
    c = lax.rem(me, 2)
    x = lax.rem(me // 2, 2)
    z = me // 4
    core_mate = me + 1 - 2 * c
    x_mate = me + 2 - 4 * x

    def local(s):
        return pltpu.make_async_copy(hidden_hbm.at[s], hid.at[s], local_sem.at[s])

    weight_copy = pltpu.make_async_copy(weight_hbm, weights, local_sem.at[steps])
    for s in range(steps):
        local(s).start()
    weight_copy.start()

    barrier = pltpu.get_barrier_semaphore()

    @pl.loop(1, n)
    def _(j):
        pl.semaphore_signal(
            barrier, inc=1, device_id={"expert": lax.rem(me + j, n)}, device_id_type=MESH
        )

    pl.semaphore_wait(barrier, n - 1)

    def remote(src, dst, send, recv, target):
        return pltpu.make_async_remote_copy(
            src_ref=src, dst_ref=dst, send_sem=send, recv_sem=recv,
            device_id={"expert": target}, device_id_type=MESH,
        )

    def hidden_to(s, target):
        return remote(
            outbox.at[s, target], inbox.at[s, me], hid_send.at[s, target], hid_recv.at[s, me], target
        )

    def hidden_from(s, source):
        return remote(
            outbox.at[s, source], inbox.at[s, source], hid_send.at[s, source],
            hid_recv.at[s, source], source,
        )

    slot = lax.broadcasted_iota(jnp.int32, (n * tok, rows), 0)
    choice = lax.broadcasted_iota(jnp.int32, (n * tok, rows), 1)
    same_token = lax.rem(slot, tok) == choice // top
    target_of = slot // tok
    for s in range(steps):
        picked = same_token & (owners_ref[s] == target_of)
        scale = jnp.sum(jnp.where(picked, gating_ref[s], 0.0), axis=1, keepdims=True)
        chosen = jnp.where(picked, 1.0, 0.0).astype(jnp.bfloat16)
        local(s).wait()
        dense = jnp.dot(chosen, hid[s], preferred_element_type=jnp.float32) * scale
        outbox[s] = dense.astype(jnp.bfloat16).reshape(n, tok, dense.shape[1])

        @pl.loop(1, n)
        def _(j):
            hidden_to(s, lax.rem(me + j, n)).start()

        inbox[s, me] = outbox[s, me]

    weight_copy.wait()
    levels = n.bit_length() - 1
    slice_rows = swap_out.shape[1]
    row = lax.broadcasted_iota(jnp.int32, (slice_rows, weights.shape[0]), 0)
    unit = lax.broadcasted_iota(jnp.int32, (slice_rows, weights.shape[0]), 1)
    handed = jnp.concatenate(
        [jnp.where(unit == row + pair_ref[s, 0] * slice_rows, 1.0, 0.0) for s in range(steps)]
    ).astype(jnp.bfloat16)

    @pl.loop(0, width // tile)
    def _(j):
        columns = pl.ds(pl.multiple_of(j * tile, tile), tile)
        block = jnp.dot(handed, weights[:, columns], preferred_element_type=jnp.float32)
        swap_out[:, :, columns] = block.astype(jnp.bfloat16).reshape(steps, slice_rows, tile)

    swaps = []
    for s in range(steps):
        stride = 2 ** (levels - 1 - s % levels)
        partner = me + stride - 2 * stride * lax.rem(me // stride, 2)
        swaps.append(
            remote(swap_out.at[s], swapped_ref.at[s, 0], swap_sem.at[0, s], swap_sem.at[1, s], partner)
        )

    def core_copy(s):
        return remote(core_out.at[s], core_in.at[s], core_sem.at[0, s], core_sem.at[1, s], core_mate)

    def x_copy(s):
        return remote(x_out.at[s], x_in.at[s], x_sem.at[0, s], x_sem.at[1, s], x_mate)

    def up_copy(s, hop):
        part = pl.ds(hop + 1, planes - 1 - hop)
        return remote(
            up_out.at[s, part], up_in.at[s, part], up_sem.at[0, s], up_sem.at[1, s], me + 4
        )

    def down_copy(s, hop):
        part = pl.ds(0, planes - 1 - hop)
        return remote(
            down_out.at[s, part], down_in.at[s, part], down_sem.at[0, s], down_sem.at[1, s], me - 4
        )

    def product(s):
        @pl.loop(1, n)
        def _(j):
            hidden_from(s, lax.rem(me + j, n)).wait_recv()

        @pl.loop(0, width // tile)
        def _(j):
            columns = pl.ds(pl.multiple_of(j * tile, tile), tile)
            block = jnp.dot(
                inbox[s].reshape(n * tok, inbox.shape[3]), weights[:, columns],
                preferred_element_type=jnp.float32,
            )
            acc[s, :, :, columns] = block.reshape(n, tok, tile)

        @pl.loop(0, n // 2)
        def _(q):
            core_out[s, q] = acc[s, 2 * q + 1 - c].astype(jnp.bfloat16)

        core_copy(s).start()

    def across_x(s):
        core_copy(s).wait_recv()

        @pl.loop(0, planes)
        def _(p):
            q = 2 * p + 1 - x
            x_out[s, p] = (acc[s, 2 * q + c] + core_in[s, q].astype(jnp.float32)).astype(jnp.bfloat16)

        x_copy(s).start()

    def plane_sum(s, p):
        q = 2 * p + x
        return (
            acc[s, 2 * q + c] + core_in[s, q].astype(jnp.float32) + x_in[s, p].astype(jnp.float32)
        )

    def along_z(s, hop):
        if hop == 0:
            x_copy(s).wait_recv()

        @pl.when(z == hop)
        def _():
            if hop:
                up_copy(s, hop - 1).wait_recv()

            @pl.loop(hop + 1, planes)
            def _(p):
                total = plane_sum(s, p)
                if hop:
                    total = total + up_in[s, p].astype(jnp.float32)
                up_out[s, p] = total.astype(jnp.bfloat16)

            up_copy(s, hop).start()

        @pl.when(z == planes - 1 - hop)
        def _():
            if hop:
                down_copy(s, hop - 1).wait_recv()

            @pl.loop(0, planes - 1 - hop)
            def _(p):
                total = plane_sum(s, p)
                if hop:
                    total = total + down_in[s, p].astype(jnp.float32)
                down_out[s, p] = total.astype(jnp.bfloat16)

            down_copy(s, hop).start()

    def finish(s):
        @pl.when(z == planes - 1)
        def _():
            up_copy(s, planes - 2).wait_recv()
            mixed_ref[s] = (plane_sum(s, z) + up_in[s, z].astype(jnp.float32)).astype(mixed_ref.dtype)

        @pl.when(z == 0)
        def _():
            down_copy(s, planes - 2).wait_recv()
            mixed_ref[s] = (plane_sum(s, z) + down_in[s, z].astype(jnp.float32)).astype(mixed_ref.dtype)

        @pl.when((z > 0) & (z < planes - 1))
        def _():
            total = plane_sum(s, z) + up_in[s, z].astype(jnp.float32) + down_in[s, z].astype(jnp.float32)
            mixed_ref[s] = total.astype(mixed_ref.dtype)

    hops = planes - 1
    for i in range(steps + hops + 1):
        if i < steps:
            product(i)
            swaps[i].start()
        for hop in range(hops - 1, 0, -1):
            if 0 <= i - 1 - hop < steps:
                along_z(i - 1 - hop, hop)
        if i < steps:
            across_x(i)
        if 0 <= i - 1 < steps:
            along_z(i - 1, 0)
        if 0 <= i - 1 - hops < steps:
            finish(i - 1 - hops)

    for s in range(steps):
        @pl.loop(1, n)
        def _(j):
            hidden_to(s, lax.rem(me + j, n)).wait_send()

        swaps[s].wait()
        core_copy(s).wait_send()
        x_copy(s).wait_send()
        for hop in range(hops):
            @pl.when(z == hop)
            def _():
                up_copy(s, hop).wait_send()

            @pl.when(z == planes - 1 - hop)
            def _():
                down_copy(s, hop).wait_send()


def kernel_device(hidden, down_weight, logits, routes, placement, pair_slice):
    steps, tok, top, hidden_cols = hidden.shape
    n = lax.axis_size("expert")
    weights = down_weight[0]
    width = weights.shape[1]
    slice_rows = weights.shape[0] // NSLICE
    expert_ids = jnp.arange(n, dtype=jnp.int32)
    owners = jnp.sum(jnp.where(routes[..., None] == expert_ids, placement, 0), axis=-1)
    scores = jax.nn.sigmoid(logits)
    gating = ROUTE_SCALE * scores / jnp.sum(scores, axis=-1, keepdims=True)
    planes = n // 4
    b16, f32 = jnp.bfloat16, jnp.float32
    dma = pltpu.SemaphoreType.DMA
    anywhere = pl.BlockSpec(memory_space=pl.ANY)
    vmem = pl.BlockSpec(memory_space=pltpu.VMEM)
    return pl.pallas_call(
        functools.partial(kernel, n),
        out_shape=(
            jax.ShapeDtypeStruct((steps, tok, width), b16),
            jax.ShapeDtypeStruct((steps, 1, slice_rows, width), b16),
        ),
        in_specs=[anywhere, anywhere, vmem, vmem, pl.BlockSpec(memory_space=pltpu.SMEM)],
        out_specs=(vmem, anywhere),
        scratch_shapes=[
            pltpu.VMEM((steps, tok * top, hidden_cols), b16),
            pltpu.VMEM(weights.shape, b16),
            pltpu.VMEM((steps, n, tok, hidden_cols), b16),
            pltpu.VMEM((steps, n, tok, hidden_cols), b16),
            pltpu.VMEM((steps, n, tok, width), f32),
            pltpu.VMEM((steps, n // 2, tok, width), b16),
            pltpu.VMEM((steps, n // 2, tok, width), b16),
            pltpu.VMEM((steps, planes, tok, width), b16),
            pltpu.VMEM((steps, planes, tok, width), b16),
            pltpu.VMEM((steps, planes, tok, width), b16),
            pltpu.VMEM((steps, planes, tok, width), b16),
            pltpu.VMEM((steps, planes, tok, width), b16),
            pltpu.VMEM((steps, planes, tok, width), b16),
            pltpu.VMEM((steps, slice_rows, width), b16),
            dma((steps + 1,)), dma((steps, n)), dma((steps, n)), dma((2, steps)), dma((2, steps)),
            dma((2, steps)), dma((2, steps)), dma((2, steps)),
        ],
        compiler_params=pltpu.CompilerParams(
            collective_id=0, has_side_effects=True, vmem_limit_bytes=VMEM_BYTES
        ),
    )(
        hidden.reshape(steps, tok * top, hidden_cols),
        weights,
        owners.reshape(steps, 1, tok * top),
        gating.reshape(steps, 1, tok * top),
        pair_slice,
    )


def per_device(hidden, down_weight, logits, routes, placement, pair_slice):
    steps, tok, top, hidden_cols = hidden.shape
    n = lax.axis_size("expert")
    width = down_weight.shape[2]
    capacity = min(tok, 2 * ((tok * top + n - 1) // n))
    held = n * tok * width * steps * 11
    fits = n % 8 == 0 and capacity == tok and lax.axis_size("sub") == 1 and held < VMEM_BYTES
    body = kernel_device if fits and width % 512 == 0 else plain_device
    return body(hidden, down_weight, logits, routes, placement, pair_slice)


def solution(mesh):
    placed = (
        P(None, ("groups", "expert"), None, "sub"),
        P("expert", None, "sub"),
        P(None, ("groups", "expert"), None),
        P(None, ("groups", "expert"), None),
        P(),
        P("groups", "expert"),
    )
    return jax.shard_map(
        per_device,
        mesh=mesh,
        in_specs=placed,
        out_specs=(P(None, ("groups", "expert"), "sub"), P("groups", "expert", None, "sub")),
        check_vma=False,
    )
```

```python
import functools
import jax
import jax.numpy as jnp
from jax import lax
from jax.experimental import pallas as pl
from jax.experimental.pallas import tpu as pltpu
from jax.sharding import PartitionSpec as P

MESH = pl.DeviceIdType.MESH
NSLICE = 32
VMEM_BYTES = 60 * 2**20
PARTS = 2
TILES = 7
DIRECT = 2
AHEAD = 4


ROUTE_SCALE = 2.5


def swapped(value, axis, stride):
    mask = 2**stride
    pairs = [(source, source ^ mask) for source in range(lax.axis_size(axis))]
    return lax.ppermute(value, axis, pairs)


def widen_rows(flat_rows):
    return lax.all_gather(flat_rows, "sub", axis=1, tiled=True)


def send_back(results):
    return lax.all_to_all(results, "expert", split_axis=0, concat_axis=0, tiled=True)


def plain_device(hidden, down_weight, logits, routes, placement, pair_slice):
    steps, tok_rows, top_count, hidden_cols = hidden.shape
    devices = lax.axis_size("expert")
    capacity = min(tok_rows, 2 * ((tok_rows * top_count + devices - 1) // devices))
    weights = down_weight[0]
    slice_rows = weights.shape[0] // NSLICE
    expert_ids = jnp.arange(devices, dtype=jnp.int32)
    owners = jnp.sum(jnp.where(routes[..., None] == expert_ids, placement, 0), axis=-1)
    owners = owners.reshape(steps, tok_rows * top_count)
    onehot = (owners[..., None] == expert_ids).astype(jnp.int32)
    earlier = jnp.cumsum(onehot, axis=1) - onehot
    slot_of = jnp.sum(earlier * onehot, axis=2)
    slot_ids = jnp.arange(capacity, dtype=jnp.int32)
    chosen = ((onehot[..., None] == 1) & (slot_of[:, :, None, None] == slot_ids)).astype(
        jnp.bfloat16
    )
    chosen = chosen.reshape(steps, tok_rows * top_count, devices * capacity)
    scores = jax.nn.sigmoid(logits)
    gating = ROUTE_SCALE * scores / jnp.sum(scores, axis=-1, keepdims=True)
    token_rows = widen_rows(hidden.reshape(-1, hidden_cols)).reshape(
        steps, tok_rows * top_count, -1
    )
    levels = devices.bit_length() - 1
    mixed_all = []
    swapped_all = []
    for step in range(steps):
        outgoing = jnp.einsum(
            "qm,qw->mw", chosen[step], token_rows[step], preferred_element_type=jnp.float32
        )
        outgoing = outgoing.astype(jnp.bfloat16).reshape(devices, capacity, -1)
        received = lax.all_to_all(outgoing, "expert", split_axis=0, concat_axis=0, tiled=True)
        source_count, slot_count, columns = received.shape
        flat_rows = received.reshape(source_count * slot_count, columns)
        results = jnp.dot(flat_rows, weights, preferred_element_type=jnp.float32).astype(
            jnp.bfloat16
        )
        returned = send_back(results.reshape(source_count, slot_count, -1))
        per_slot = jnp.dot(
            chosen[step],
            returned.reshape(devices * capacity, -1),
            preferred_element_type=jnp.float32,
        )
        weighted = gating[step][..., None] * per_slot.reshape(tok_rows, top_count, -1)
        mixed_all.append(jnp.sum(weighted, axis=1).astype(jnp.bfloat16))
        swap_bit = levels - 1 - step % levels
        start_row = pair_slice[step, 0] * slice_rows
        own_slice = lax.dynamic_slice_in_dim(weights, start_row, slice_rows, 0)
        traded = swapped(own_slice, "expert", swap_bit)
        swapped_all.append(traded[None])
    return (jnp.stack(mixed_all), jnp.stack(swapped_all))


def kernel(
    n, hidden_hbm, weight_hbm, logits_ref, routes_ref, placement_ref, pair_ref, mixed_ref, swapped_ref,
    hid, weights, outbox, inbox, acc, core_out, core_in, x_out, x_in,
    up_out, up_in, down_out, down_in, swap_out,
    local_sem, hid_send, hid_recv, core_sem, x_sem, up_sem, down_sem, plane_sem, swap_sem,
):
    steps = hid.shape[0]
    rows = hid.shape[1]
    tok = inbox.shape[2]
    top = rows // tok
    width = acc.shape[3]
    parts = weights.shape[1] // width
    tile = width // TILES
    planes = n // 4
    me = lax.axis_index("expert")
    c = lax.rem(me, 2)
    x = lax.rem(me // 2, 2)
    z = me // 4
    core_mate = me + 1 - 2 * c
    x_mate = me + 2 - 4 * x

    def local(s):
        return pltpu.make_async_copy(hidden_hbm.at[s], hid.at[s], local_sem.at[s])

    weight_copy = pltpu.make_async_copy(weight_hbm, weights, local_sem.at[steps])
    for s in range(steps):
        local(s).start()
    weight_copy.start()
    barrier = pltpu.get_barrier_semaphore()

    @pl.loop(1, n)
    def _(j):
        pl.semaphore_signal(
            barrier, inc=1, device_id={"expert": lax.rem(me + j, n)}, device_id_type=MESH
        )

    def remote(src, dst, send, recv, target):
        return pltpu.make_async_remote_copy(
            src_ref=src, dst_ref=dst, send_sem=send, recv_sem=recv,
            device_id={"expert": target}, device_id_type=MESH,
        )

    def hidden_to(s, target):
        return remote(
            outbox.at[s, target], inbox.at[s, me], hid_send.at[s, target], hid_recv.at[s, me], target
        )

    def hidden_from(s, source):
        return remote(
            outbox.at[s, source], inbox.at[s, source], hid_send.at[s, source],
            hid_recv.at[s, source], source,
        )

    f32 = jnp.float32
    token = lax.broadcasted_iota(jnp.int32, (tok, rows), 0)
    choice = lax.broadcasted_iota(jnp.int32, (tok, rows), 1)
    spread = jnp.where(choice // top == token, 1.0, 0.0)
    kth = lax.broadcasted_iota(jnp.int32, (top, rows), 0)
    of_kth = lax.rem(lax.broadcasted_iota(jnp.int32, (top, rows), 1), top) == kth

    def in_row(values):
        wide = jnp.dot(
            values, spread, precision=lax.Precision.HIGHEST, preferred_element_type=f32
        )
        return jnp.sum(jnp.where(of_kth, wide, 0.0), axis=0, keepdims=True)

    slot = lax.broadcasted_iota(jnp.int32, (n * tok, rows), 0)
    column = lax.broadcasted_iota(jnp.int32, (n * tok, rows), 1)
    same_token = lax.rem(slot, tok) == column // top
    target_of = (slot // tok).astype(f32)

    def prepare(s):
        scores = jax.nn.sigmoid(logits_ref[s])
        gating = in_row(ROUTE_SCALE * scores / jnp.sum(scores, axis=0, keepdims=True))
        routes = routes_ref[s]
        owners = jnp.zeros((top, tok), jnp.int32)
        for e in range(n):
            owners = jnp.where(routes == e, placement_ref[e], owners)
        picked = same_token & (in_row(owners.astype(f32)) == target_of)
        scale = jnp.sum(jnp.where(picked, gating, 0.0), axis=1, keepdims=True)
        chosen = jnp.where(picked, 1.0, 0.0).astype(jnp.bfloat16)
        local(s).wait()
        dense = jnp.dot(chosen, hid[s], preferred_element_type=f32) * scale
        outbox[s] = dense.astype(jnp.bfloat16).reshape(n, tok, dense.shape[1])
        inbox[s, me] = outbox[s, me]

    def send_hidden(s):
        @pl.loop(1, n)
        def _(j):
            hidden_to(s, lax.rem(me + j, n)).start()

    prepare(0)
    pl.semaphore_wait(barrier, n - 1)
    send_hidden(0)
    for s in range(1, steps):
        prepare(s)
        if s < AHEAD:
            send_hidden(s)

    weight_copy.wait()
    levels = n.bit_length() - 1
    slice_rows = swap_out.shape[1]
    row = lax.broadcasted_iota(jnp.int32, (slice_rows, weights.shape[0]), 0)
    unit = lax.broadcasted_iota(jnp.int32, (slice_rows, weights.shape[0]), 1)
    handed = jnp.concatenate(
        [jnp.where(unit == row + pair_ref[0, s] * slice_rows, 1.0, 0.0) for s in range(steps)]
    ).astype(jnp.bfloat16)

    @pl.loop(0, parts * TILES)
    def _(j):
        columns = pl.ds(pl.multiple_of(j * tile, tile), tile)
        block = jnp.dot(handed, weights[:, columns], preferred_element_type=jnp.float32)
        swap_out[:, :, columns] = block.astype(jnp.bfloat16).reshape(steps, slice_rows, tile)

    swaps = []
    for s in range(steps):
        stride = 2 ** (levels - 1 - s % levels)
        partner = me + stride - 2 * stride * lax.rem(me // stride, 2)
        swaps.append(
            remote(swap_out.at[s], swapped_ref.at[s, 0], swap_sem.at[0, s], swap_sem.at[1, s], partner)
        )

    def core_copy(s):
        return remote(core_out.at[s], core_in.at[s], core_sem.at[0, s], core_sem.at[1, s], core_mate)

    def x_copy(s):
        return remote(x_out.at[s], x_in.at[s], x_sem.at[0, s], x_sem.at[1, s], x_mate)

    def up_copy(s, hop):
        part = pl.ds(hop + 1, planes - 1 - hop)
        return remote(
            up_out.at[s, part], up_in.at[s, part], up_sem.at[0, s], up_sem.at[1, s], me + 4
        )

    def down_copy(s, hop):
        part = pl.ds(0, planes - 1 - hop)
        return remote(
            down_out.at[s, part], down_in.at[s, part], down_sem.at[0, s], down_sem.at[1, s], me - 4
        )

    def arrive(s):
        @pl.loop(1, n)
        def _(j):
            hidden_from(s, lax.rem(me + j, n)).wait_recv()

    def product(s):
        base = s % parts * width

        @pl.loop(0, TILES)
        def _(j):
            columns = pl.ds(pl.multiple_of(j * tile, tile), tile)
            block = jnp.dot(
                inbox[s // parts].reshape(n * tok, inbox.shape[3]),
                weights[:, pl.ds(pl.multiple_of(base + j * tile, tile), tile)],
                preferred_element_type=f32,
            )
            acc[s, :, :, columns] = block.reshape(n, tok, tile)

        @pl.loop(0, n // 2)
        def _(q):
            core_out[s, q] = acc[s, 2 * q + 1 - c].astype(jnp.bfloat16)

        core_copy(s).start()

    def across_x(s):
        core_copy(s).wait_recv()

        @pl.loop(0, planes)
        def _(p):
            q = 2 * p + 1 - x
            x_out[s, p] = (acc[s, 2 * q + c] + core_in[s, q].astype(jnp.float32)).astype(jnp.bfloat16)

        x_copy(s).start()

    def plane_sum(s, p):
        q = 2 * p + x
        return (
            acc[s, 2 * q + c] + core_in[s, q].astype(jnp.float32) + x_in[s, p].astype(jnp.float32)
        )

    def along_z(s, hop):
        if hop == 0:
            x_copy(s).wait_recv()

        @pl.when(z == hop)
        def _():
            if hop:
                up_copy(s, hop - 1).wait_recv()

            @pl.loop(hop + 1, planes)
            def _(p):
                total = plane_sum(s, p)
                if hop:
                    total = total + up_in[s, p].astype(jnp.float32)
                up_out[s, p] = total.astype(jnp.bfloat16)

            up_copy(s, hop).start()

        @pl.when(z == planes - 1 - hop)
        def _():
            if hop:
                down_copy(s, hop - 1).wait_recv()

            @pl.loop(0, planes - 1 - hop)
            def _(p):
                total = plane_sum(s, p)
                if hop:
                    total = total + down_in[s, p].astype(jnp.float32)
                down_out[s, p] = total.astype(jnp.bfloat16)

            down_copy(s, hop).start()

    def plane_to(s, p):
        return remote(
            up_out.at[s, p], up_in.at[s, z], plane_sem.at[0, s, p], plane_sem.at[1, s, z],
            me + 4 * (p - z),
        )

    def plane_from(s, p):
        return remote(
            up_out.at[s, p], up_in.at[s, p], plane_sem.at[0, s, p], plane_sem.at[1, s, p],
            me + 4 * (p - z),
        )

    def to_planes(s):
        x_copy(s).wait_recv()

        @pl.loop(1, planes)
        def _(j):
            p = lax.rem(z + j, planes)
            up_out[s, p] = plane_sum(s, p).astype(jnp.bfloat16)
            plane_to(s, p).start()

    def finish_direct(s):
        @pl.loop(1, planes)
        def _(j):
            plane_from(s, lax.rem(z + j, planes)).wait_recv()

        total = plane_sum(s, z)
        for j in range(1, planes):
            total = total + up_in[s, lax.rem(z + j, planes)].astype(f32)
        mixed_ref[s // parts, :, pl.ds(s % parts * width, width)] = total.astype(mixed_ref.dtype)

    def finish(s):
        columns = pl.ds(s % parts * width, width)

        def put(total):
            mixed_ref[s // parts, :, columns] = total.astype(mixed_ref.dtype)

        @pl.when(z == planes - 1)
        def _():
            up_copy(s, planes - 2).wait_recv()
            put(plane_sum(s, z) + up_in[s, z].astype(f32))

        @pl.when(z == 0)
        def _():
            down_copy(s, planes - 2).wait_recv()
            put(plane_sum(s, z) + down_in[s, z].astype(f32))

        @pl.when((z > 0) & (z < planes - 1))
        def _():
            put(plane_sum(s, z) + up_in[s, z].astype(f32) + down_in[s, z].astype(f32))

    hops = planes - 1
    chunks = steps * parts
    chained = chunks - DIRECT
    last_arrival = chunks - parts
    for s in range(steps):
        if s % levels >= levels - 2:
            swaps[s].start()
    for i in range(chunks + hops + 1):
        if i < chunks:
            if i % parts == 0:
                arrive(i // parts)
                if i // parts + AHEAD < steps:
                    send_hidden(i // parts + AHEAD)
            product(i)
            if i == last_arrival:
                for s in range(steps):
                    if s % levels < levels - 2:
                        swaps[s].start()
        for hop in range(hops - 1, 0, -1):
            if 0 <= i - 1 - hop < chained:
                along_z(i - 1 - hop, hop)
        if i < chunks:
            across_x(i)
        if 0 <= i - 1 < chained:
            along_z(i - 1, 0)
        if chained <= i - 1 < chunks:
            to_planes(i - 1)
        if 0 <= i - 1 - hops < chained:
            finish(i - 1 - hops)
    for s in range(chained, chunks):
        finish_direct(s)

    for s in range(steps):
        @pl.loop(1, n)
        def _(j):
            hidden_to(s, lax.rem(me + j, n)).wait_send()

        swaps[s].wait()
    for s in range(chunks):
        core_copy(s).wait_send()
        x_copy(s).wait_send()
        if s >= chained:
            @pl.loop(1, planes)
            def _(j):
                plane_to(s, lax.rem(z + j, planes)).wait_send()

            continue
        for hop in range(hops):
            @pl.when(z == hop)
            def _():
                up_copy(s, hop).wait_send()

            @pl.when(z == planes - 1 - hop)
            def _():
                down_copy(s, hop).wait_send()


def kernel_device(hidden, down_weight, logits, routes, placement, pair_slice):
    steps, tok, top, hidden_cols = hidden.shape
    n = lax.axis_size("expert")
    weights = down_weight[0]
    width = weights.shape[1]
    slice_rows = weights.shape[0] // NSLICE
    planes = n // 4
    b16, f32 = jnp.bfloat16, jnp.float32
    dma = pltpu.SemaphoreType.DMA
    anywhere = pl.BlockSpec(memory_space=pl.ANY)
    vmem = pl.BlockSpec(memory_space=pltpu.VMEM)
    smem = pl.BlockSpec(memory_space=pltpu.SMEM)
    chunks, part = steps * PARTS, width // PARTS
    return pl.pallas_call(
        functools.partial(kernel, n),
        out_shape=(
            jax.ShapeDtypeStruct((steps, tok, width), b16),
            jax.ShapeDtypeStruct((steps, 1, slice_rows, width), b16),
        ),
        in_specs=[anywhere, anywhere, vmem, vmem, smem, smem],
        out_specs=(vmem, anywhere),
        scratch_shapes=[
            pltpu.VMEM((steps, tok * top, hidden_cols), b16),
            pltpu.VMEM(weights.shape, b16),
            pltpu.VMEM((steps, n, tok, hidden_cols), b16),
            pltpu.VMEM((steps, n, tok, hidden_cols), b16),
            pltpu.VMEM((chunks, n, tok, part), f32),
            pltpu.VMEM((chunks, n // 2, tok, part), b16),
            pltpu.VMEM((chunks, n // 2, tok, part), b16),
            pltpu.VMEM((chunks, planes, tok, part), b16),
            pltpu.VMEM((chunks, planes, tok, part), b16),
            pltpu.VMEM((chunks, planes, tok, part), b16),
            pltpu.VMEM((chunks, planes, tok, part), b16),
            pltpu.VMEM((chunks, planes, tok, part), b16),
            pltpu.VMEM((chunks, planes, tok, part), b16),
            pltpu.VMEM((steps, slice_rows, width), b16),
            dma((steps + 1,)), dma((steps, n)), dma((steps, n)), dma((2, chunks)), dma((2, chunks)),
            dma((2, chunks)), dma((2, chunks)), dma((2, chunks, planes)),
            dma((2, steps)),
        ],
        compiler_params=pltpu.CompilerParams(
            collective_id=0, has_side_effects=True, vmem_limit_bytes=VMEM_BYTES
        ),
    )(
        hidden.reshape(steps, tok * top, hidden_cols),
        weights,
        logits.transpose(0, 2, 1),
        routes.transpose(0, 2, 1),
        placement,
        pair_slice.T,
    )


def per_device(hidden, down_weight, logits, routes, placement, pair_slice):
    steps, tok, top, hidden_cols = hidden.shape
    n = lax.axis_size("expert")
    width = down_weight.shape[2]
    capacity = min(tok, 2 * ((tok * top + n - 1) // n))
    held = n * tok * width * steps * 11
    fits = n % 8 == 0 and capacity == tok and lax.axis_size("sub") == 1 and held < VMEM_BYTES
    body = kernel_device if fits and width % (128 * PARTS * TILES) == 0 else plain_device
    return body(hidden, down_weight, logits, routes, placement, pair_slice)


def solution(mesh):
    placed = (
        P(None, ("groups", "expert"), None, "sub"),
        P("expert", None, "sub"),
        P(None, ("groups", "expert"), None),
        P(None, ("groups", "expert"), None),
        P(),
        P("groups", "expert"),
    )
    return jax.shard_map(
        per_device,
        mesh=mesh,
        in_specs=placed,
        out_specs=(P(None, ("groups", "expert"), "sub"), P("groups", "expert", None, "sub")),
        check_vma=False,
    )
```

```python
import functools
import jax
import jax.numpy as jnp
from jax import lax
from jax.experimental import pallas as pl
from jax.experimental.pallas import tpu as pltpu
from jax.sharding import PartitionSpec as P

MESH = pl.DeviceIdType.MESH
NSLICE = 32
VMEM_BYTES = 60 * 2**20
PARTS = 2
TILES = 7
DIRECT = 2
AHEAD = 1


ROUTE_SCALE = 2.5


def swapped(value, axis, stride):
    mask = 2**stride
    pairs = [(source, source ^ mask) for source in range(lax.axis_size(axis))]
    return lax.ppermute(value, axis, pairs)


def widen_rows(flat_rows):
    return lax.all_gather(flat_rows, "sub", axis=1, tiled=True)


def send_back(results):
    return lax.all_to_all(results, "expert", split_axis=0, concat_axis=0, tiled=True)


def plain_device(hidden, down_weight, logits, routes, placement, pair_slice):
    steps, tok_rows, top_count, hidden_cols = hidden.shape
    devices = lax.axis_size("expert")
    capacity = min(tok_rows, 2 * ((tok_rows * top_count + devices - 1) // devices))
    weights = down_weight[0]
    slice_rows = weights.shape[0] // NSLICE
    expert_ids = jnp.arange(devices, dtype=jnp.int32)
    owners = jnp.sum(jnp.where(routes[..., None] == expert_ids, placement, 0), axis=-1)
    owners = owners.reshape(steps, tok_rows * top_count)
    onehot = (owners[..., None] == expert_ids).astype(jnp.int32)
    earlier = jnp.cumsum(onehot, axis=1) - onehot
    slot_of = jnp.sum(earlier * onehot, axis=2)
    slot_ids = jnp.arange(capacity, dtype=jnp.int32)
    chosen = ((onehot[..., None] == 1) & (slot_of[:, :, None, None] == slot_ids)).astype(
        jnp.bfloat16
    )
    chosen = chosen.reshape(steps, tok_rows * top_count, devices * capacity)
    scores = jax.nn.sigmoid(logits)
    gating = ROUTE_SCALE * scores / jnp.sum(scores, axis=-1, keepdims=True)
    token_rows = widen_rows(hidden.reshape(-1, hidden_cols)).reshape(
        steps, tok_rows * top_count, -1
    )
    levels = devices.bit_length() - 1
    mixed_all = []
    swapped_all = []
    for step in range(steps):
        outgoing = jnp.einsum(
            "qm,qw->mw", chosen[step], token_rows[step], preferred_element_type=jnp.float32
        )
        outgoing = outgoing.astype(jnp.bfloat16).reshape(devices, capacity, -1)
        received = lax.all_to_all(outgoing, "expert", split_axis=0, concat_axis=0, tiled=True)
        source_count, slot_count, columns = received.shape
        flat_rows = received.reshape(source_count * slot_count, columns)
        results = jnp.dot(flat_rows, weights, preferred_element_type=jnp.float32).astype(
            jnp.bfloat16
        )
        returned = send_back(results.reshape(source_count, slot_count, -1))
        per_slot = jnp.dot(
            chosen[step],
            returned.reshape(devices * capacity, -1),
            preferred_element_type=jnp.float32,
        )
        weighted = gating[step][..., None] * per_slot.reshape(tok_rows, top_count, -1)
        mixed_all.append(jnp.sum(weighted, axis=1).astype(jnp.bfloat16))
        swap_bit = levels - 1 - step % levels
        start_row = pair_slice[step, 0] * slice_rows
        own_slice = lax.dynamic_slice_in_dim(weights, start_row, slice_rows, 0)
        traded = swapped(own_slice, "expert", swap_bit)
        swapped_all.append(traded[None])
    return (jnp.stack(mixed_all), jnp.stack(swapped_all))


def kernel(
    n, hidden_hbm, weight_hbm, logits_ref, routes_ref, placement_ref, pair_ref, mixed_ref, swapped_ref,
    hid, weights, outbox, inbox, acc, core_out, core_in, x_out, x_in,
    up_out, up_in, down_out, down_in, swap_out,
    local_sem, hid_send, hid_recv, core_sem, x_sem, up_sem, down_sem, plane_sem, swap_sem,
):
    steps = hid.shape[0]
    rows = hid.shape[1]
    tok = inbox.shape[2]
    top = rows // tok
    width = acc.shape[3]
    parts = weights.shape[1] // width
    tile = width // TILES
    planes = n // 4
    me = lax.axis_index("expert")
    c = lax.rem(me, 2)
    x = lax.rem(me // 2, 2)
    z = me // 4
    core_mate = me + 1 - 2 * c
    x_mate = me + 2 - 4 * x

    def local(s):
        return pltpu.make_async_copy(hidden_hbm.at[s], hid.at[s], local_sem.at[s])

    weight_copy = pltpu.make_async_copy(weight_hbm, weights, local_sem.at[steps])
    for s in range(steps):
        local(s).start()
    weight_copy.start()
    barrier = pltpu.get_barrier_semaphore()

    @pl.loop(1, n)
    def _(j):
        pl.semaphore_signal(
            barrier, inc=1, device_id={"expert": lax.rem(me + j, n)}, device_id_type=MESH
        )

    def remote(src, dst, send, recv, target):
        return pltpu.make_async_remote_copy(
            src_ref=src, dst_ref=dst, send_sem=send, recv_sem=recv,
            device_id={"expert": target}, device_id_type=MESH,
        )

    def hidden_to(s, target):
        return remote(
            outbox.at[s, target], inbox.at[s, me], hid_send.at[s, target], hid_recv.at[s, me], target
        )

    def hidden_from(s, source):
        return remote(
            outbox.at[s, source], inbox.at[s, source], hid_send.at[s, source],
            hid_recv.at[s, source], source,
        )

    f32 = jnp.float32
    token = lax.broadcasted_iota(jnp.int32, (tok, rows), 0)
    choice = lax.broadcasted_iota(jnp.int32, (tok, rows), 1)
    spread = jnp.where(choice // top == token, 1.0, 0.0)
    kth = lax.broadcasted_iota(jnp.int32, (top, rows), 0)
    of_kth = lax.rem(lax.broadcasted_iota(jnp.int32, (top, rows), 1), top) == kth

    def in_row(values):
        wide = jnp.dot(
            values, spread, precision=lax.Precision.HIGHEST, preferred_element_type=f32
        )
        return jnp.sum(jnp.where(of_kth, wide, 0.0), axis=0, keepdims=True)

    slot = lax.broadcasted_iota(jnp.int32, (n * tok, rows), 0)
    column = lax.broadcasted_iota(jnp.int32, (n * tok, rows), 1)
    same_token = lax.rem(slot, tok) == column // top
    target_of = (slot // tok).astype(f32)

    def prepare(s):
        scores = jax.nn.sigmoid(logits_ref[s])
        gating = in_row(ROUTE_SCALE * scores / jnp.sum(scores, axis=0, keepdims=True))
        routes = routes_ref[s]
        owners = jnp.zeros((top, tok), jnp.int32)
        for e in range(n):
            owners = jnp.where(routes == e, placement_ref[e], owners)
        picked = same_token & (in_row(owners.astype(f32)) == target_of)
        scale = jnp.sum(jnp.where(picked, gating, 0.0), axis=1, keepdims=True)
        chosen = jnp.where(picked, 1.0, 0.0).astype(jnp.bfloat16)
        local(s).wait()
        dense = jnp.dot(chosen, hid[s], preferred_element_type=f32) * scale
        outbox[s] = dense.astype(jnp.bfloat16).reshape(n, tok, dense.shape[1])
        inbox[s, me] = outbox[s, me]

    def send_hidden(s):
        @pl.loop(1, n)
        def _(j):
            hidden_to(s, lax.rem(me + j, n)).start()

    prepare(0)
    pl.semaphore_wait(barrier, n - 1)
    send_hidden(0)
    for s in range(1, steps):
        prepare(s)
        if s < AHEAD:
            send_hidden(s)

    weight_copy.wait()
    levels = n.bit_length() - 1
    slice_rows = swap_out.shape[1]
    row = lax.broadcasted_iota(jnp.int32, (slice_rows, weights.shape[0]), 0)
    unit = lax.broadcasted_iota(jnp.int32, (slice_rows, weights.shape[0]), 1)
    handed = jnp.concatenate(
        [jnp.where(unit == row + pair_ref[0, s] * slice_rows, 1.0, 0.0) for s in range(steps)]
    ).astype(jnp.bfloat16)

    @pl.loop(0, parts * TILES)
    def _(j):
        columns = pl.ds(pl.multiple_of(j * tile, tile), tile)
        block = jnp.dot(handed, weights[:, columns], preferred_element_type=jnp.float32)
        swap_out[:, :, columns] = block.astype(jnp.bfloat16).reshape(steps, slice_rows, tile)

    swaps = []
    for s in range(steps):
        stride = 2 ** (levels - 1 - s % levels)
        partner = me + stride - 2 * stride * lax.rem(me // stride, 2)
        swaps.append(
            remote(swap_out.at[s], swapped_ref.at[s, 0], swap_sem.at[0, s], swap_sem.at[1, s], partner)
        )

    def core_copy(s):
        return remote(core_out.at[s], core_in.at[s], core_sem.at[0, s], core_sem.at[1, s], core_mate)

    def x_copy(s):
        return remote(x_out.at[s], x_in.at[s], x_sem.at[0, s], x_sem.at[1, s], x_mate)

    def up_copy(s, hop):
        part = pl.ds(hop + 1, planes - 1 - hop)
        return remote(
            up_out.at[s, part], up_in.at[s, part], up_sem.at[0, s], up_sem.at[1, s], me + 4
        )

    def down_copy(s, hop):
        part = pl.ds(0, planes - 1 - hop)
        return remote(
            down_out.at[s, part], down_in.at[s, part], down_sem.at[0, s], down_sem.at[1, s], me - 4
        )

    def arrive(s):
        @pl.loop(1, n)
        def _(j):
            hidden_from(s, lax.rem(me + j, n)).wait_recv()

    def product(s):
        base = s % parts * width

        @pl.loop(0, TILES)
        def _(j):
            columns = pl.ds(pl.multiple_of(j * tile, tile), tile)
            block = jnp.dot(
                inbox[s // parts].reshape(n * tok, inbox.shape[3]),
                weights[:, pl.ds(pl.multiple_of(base + j * tile, tile), tile)],
                preferred_element_type=f32,
            )
            acc[s, :, :, columns] = block.reshape(n, tok, tile)

        @pl.loop(0, n // 2)
        def _(q):
            core_out[s, q] = acc[s, 2 * q + 1 - c].astype(jnp.bfloat16)

        core_copy(s).start()

    def across_x(s):
        core_copy(s).wait_recv()

        @pl.loop(0, planes)
        def _(p):
            q = 2 * p + 1 - x
            x_out[s, p] = (acc[s, 2 * q + c] + core_in[s, q].astype(jnp.float32)).astype(jnp.bfloat16)

        x_copy(s).start()

    def plane_sum(s, p):
        q = 2 * p + x
        return (
            acc[s, 2 * q + c] + core_in[s, q].astype(jnp.float32) + x_in[s, p].astype(jnp.float32)
        )

    def along_z(s, hop):
        if hop == 0:
            x_copy(s).wait_recv()

        @pl.when(z == hop)
        def _():
            if hop:
                up_copy(s, hop - 1).wait_recv()

            @pl.loop(hop + 1, planes)
            def _(p):
                total = plane_sum(s, p)
                if hop:
                    total = total + up_in[s, p].astype(jnp.float32)
                up_out[s, p] = total.astype(jnp.bfloat16)

            up_copy(s, hop).start()

        @pl.when(z == planes - 1 - hop)
        def _():
            if hop:
                down_copy(s, hop - 1).wait_recv()

            @pl.loop(0, planes - 1 - hop)
            def _(p):
                total = plane_sum(s, p)
                if hop:
                    total = total + down_in[s, p].astype(jnp.float32)
                down_out[s, p] = total.astype(jnp.bfloat16)

            down_copy(s, hop).start()

    def plane_to(s, p):
        return remote(
            up_out.at[s, p], up_in.at[s, z], plane_sem.at[0, s, p], plane_sem.at[1, s, z],
            me + 4 * (p - z),
        )

    def plane_from(s, p):
        return remote(
            up_out.at[s, p], up_in.at[s, p], plane_sem.at[0, s, p], plane_sem.at[1, s, p],
            me + 4 * (p - z),
        )

    def to_planes(s):
        x_copy(s).wait_recv()

        @pl.loop(1, planes)
        def _(j):
            p = lax.rem(z + j, planes)
            up_out[s, p] = plane_sum(s, p).astype(jnp.bfloat16)
            plane_to(s, p).start()

    def finish_direct(s):
        @pl.loop(1, planes)
        def _(j):
            plane_from(s, lax.rem(z + j, planes)).wait_recv()

        total = plane_sum(s, z)
        for j in range(1, planes):
            total = total + up_in[s, lax.rem(z + j, planes)].astype(f32)
        mixed_ref[s // parts, :, pl.ds(s % parts * width, width)] = total.astype(mixed_ref.dtype)

    def finish(s):
        columns = pl.ds(s % parts * width, width)

        def put(total):
            mixed_ref[s // parts, :, columns] = total.astype(mixed_ref.dtype)

        @pl.when(z == planes - 1)
        def _():
            up_copy(s, planes - 2).wait_recv()
            put(plane_sum(s, z) + up_in[s, z].astype(f32))

        @pl.when(z == 0)
        def _():
            down_copy(s, planes - 2).wait_recv()
            put(plane_sum(s, z) + down_in[s, z].astype(f32))

        @pl.when((z > 0) & (z < planes - 1))
        def _():
            put(plane_sum(s, z) + up_in[s, z].astype(f32) + down_in[s, z].astype(f32))

    hops = planes - 1
    chunks = steps * parts
    chained = chunks - DIRECT
    last_arrival = chunks - parts
    for s in range(steps):
        if s % levels >= levels - 2:
            swaps[s].start()
    for i in range(chunks + hops + 1):
        if i < chunks:
            if i % parts == 0:
                arrive(i // parts)
                if i // parts + AHEAD < steps:
                    send_hidden(i // parts + AHEAD)
            product(i)
            if i == last_arrival:
                for s in range(steps):
                    if s % levels < levels - 2:
                        swaps[s].start()
        for hop in range(hops - 1, 0, -1):
            if 0 <= i - 1 - hop < chained:
                along_z(i - 1 - hop, hop)
        if i < chunks:
            across_x(i)
        if 0 <= i - 1 < chained:
            along_z(i - 1, 0)
        if chained <= i - 1 < chunks:
            to_planes(i - 1)
        if 0 <= i - 1 - hops < chained:
            finish(i - 1 - hops)
    for s in range(chained, chunks):
        finish_direct(s)

    for s in range(steps):
        @pl.loop(1, n)
        def _(j):
            hidden_to(s, lax.rem(me + j, n)).wait_send()

        swaps[s].wait()
    for s in range(chunks):
        core_copy(s).wait_send()
        x_copy(s).wait_send()
        if s >= chained:
            @pl.loop(1, planes)
            def _(j):
                plane_to(s, lax.rem(z + j, planes)).wait_send()

            continue
        for hop in range(hops):
            @pl.when(z == hop)
            def _():
                up_copy(s, hop).wait_send()

            @pl.when(z == planes - 1 - hop)
            def _():
                down_copy(s, hop).wait_send()


def kernel_device(hidden, down_weight, logits, routes, placement, pair_slice):
    steps, tok, top, hidden_cols = hidden.shape
    n = lax.axis_size("expert")
    weights = down_weight[0]
    width = weights.shape[1]
    slice_rows = weights.shape[0] // NSLICE
    planes = n // 4
    b16, f32 = jnp.bfloat16, jnp.float32
    dma = pltpu.SemaphoreType.DMA
    anywhere = pl.BlockSpec(memory_space=pl.ANY)
    vmem = pl.BlockSpec(memory_space=pltpu.VMEM)
    smem = pl.BlockSpec(memory_space=pltpu.SMEM)
    chunks, part = steps * PARTS, width // PARTS
    return pl.pallas_call(
        functools.partial(kernel, n),
        out_shape=(
            jax.ShapeDtypeStruct((steps, tok, width), b16),
            jax.ShapeDtypeStruct((steps, 1, slice_rows, width), b16),
        ),
        in_specs=[anywhere, anywhere, vmem, vmem, smem, smem],
        out_specs=(vmem, anywhere),
        scratch_shapes=[
            pltpu.VMEM((steps, tok * top, hidden_cols), b16),
            pltpu.VMEM(weights.shape, b16),
            pltpu.VMEM((steps, n, tok, hidden_cols), b16),
            pltpu.VMEM((steps, n, tok, hidden_cols), b16),
            pltpu.VMEM((chunks, n, tok, part), f32),
            pltpu.VMEM((chunks, n // 2, tok, part), b16),
            pltpu.VMEM((chunks, n // 2, tok, part), b16),
            pltpu.VMEM((chunks, planes, tok, part), b16),
            pltpu.VMEM((chunks, planes, tok, part), b16),
            pltpu.VMEM((chunks, planes, tok, part), b16),
            pltpu.VMEM((chunks, planes, tok, part), b16),
            pltpu.VMEM((chunks, planes, tok, part), b16),
            pltpu.VMEM((chunks, planes, tok, part), b16),
            pltpu.VMEM((steps, slice_rows, width), b16),
            dma((steps + 1,)), dma((steps, n)), dma((steps, n)), dma((2, chunks)), dma((2, chunks)),
            dma((2, chunks)), dma((2, chunks)), dma((2, chunks, planes)),
            dma((2, steps)),
        ],
        compiler_params=pltpu.CompilerParams(
            collective_id=0, has_side_effects=True, vmem_limit_bytes=VMEM_BYTES
        ),
    )(
        hidden.reshape(steps, tok * top, hidden_cols),
        weights,
        logits.transpose(0, 2, 1),
        routes.transpose(0, 2, 1),
        placement,
        pair_slice.T,
    )


def per_device(hidden, down_weight, logits, routes, placement, pair_slice):
    steps, tok, top, hidden_cols = hidden.shape
    n = lax.axis_size("expert")
    width = down_weight.shape[2]
    capacity = min(tok, 2 * ((tok * top + n - 1) // n))
    held = n * tok * width * steps * 11
    fits = n % 8 == 0 and capacity == tok and lax.axis_size("sub") == 1 and held < VMEM_BYTES
    body = kernel_device if fits and width % (128 * PARTS * TILES) == 0 else plain_device
    return body(hidden, down_weight, logits, routes, placement, pair_slice)


def solution(mesh):
    placed = (
        P(None, ("groups", "expert"), None, "sub"),
        P("expert", None, "sub"),
        P(None, ("groups", "expert"), None),
        P(None, ("groups", "expert"), None),
        P(),
        P("groups", "expert"),
    )
    return jax.shard_map(
        per_device,
        mesh=mesh,
        in_specs=placed,
        out_specs=(P(None, ("groups", "expert"), "sub"), P("groups", "expert", None, "sub")),
        check_vma=False,
    )
```
